512 devices in a mesh: sec: 16 (over y_lo, x, core), sp: 16 (over z), tp: 2 (over y_hi).
Axes of the slice: x: 4, y: 4 (y_hi: 2, y_lo: 2; y = y_hi * 2 + y_lo), z: 16, core: 2. Of those that a mesh axis runs over, the one named last changes fastest.
Arguments:
- text_hidden: bfloat16 [32, 256, 3072], P('sec', 'sp', 'tp'), may hold values from -6 to 6
- text_qkv_weight: bfloat16 [3072, 16, 384], P('tp', 'sp'), may hold values from -0.109375 to 0.109375
- image_qkv: bfloat16 [32, 2048, 16, 384], P(('sec', 'tp'), 'sp'), may hold values from -8 to 8
- mod_weight: float32 [256, 16, 128], P(None, 'sp'), may hold values from -0.375 to 0.375
- lengths: int32 [32], P(('sec', 'tp')), may hold values from 32 to 256
- timesteps: int32 [32], P(('sec', 'tp')), may hold values from 0 to 999
Outputs:
- image_out: bfloat16 [32, 2048, 16, 128], P(('sec', 'tp'), 'sp')
- text_out: bfloat16 [32, 256, 16, 128], P(('sec', 'tp'), None, 'sp')
The draws below stay inside these ranges and needn't reach their ends.
All inputs are finite; a program needn't handle non-finite values.
Results may differ from the reference program's by a relative error of at most 0.0077.
Values may be sent and summed in bfloat16 or wider, within the bound.
No kernel may reach another device: no remote copies, remote signals or barrier semaphores. Data moves between devices by JAX's collectives and lax.ppermute only.
A program may use at most 64 MiB of HBM per device.

```python
import math
import jax
import jax.numpy as jnp
from jax import lax

D = 3072
HEADS = 16
HS = 128
FREQ = 256
TXT = 256
IMG = 2048
SAMPLES = 32
N_SEC = 16
N_TP = 2


def draw_lengths(key, part):
    key = jax.random.fold_in(key, 11)
    drawn = jax.random.randint(key, (SAMPLES,), TXT // 8, TXT + 1)
    index_row = jnp.arange(SAMPLES)
    return jnp.where(index_row == 0, TXT, jnp.where(index_row == 1, TXT // 8, drawn)).astype(jnp.int32)


def draw_image_qkv(key, part):
    key = jax.random.fold_in(key, 23)
    full_shape = (SAMPLES, IMG, HEADS, 3 * HS)
    return jnp.clip(jax.random.normal(key, full_shape, jnp.float32), -6.0, 6.0).astype(jnp.bfloat16)


def place_ends(result, own_key, smallest, high):
    spot = [jax.random.randint(jax.random.fold_in(own_key, axis), (), 0, length) for axis, length in enumerate(result.shape)]
    main_axis = result.shape.index(max(result.shape))
    next_to = spot[:main_axis] + [(spot[main_axis] + 1) % result.shape[main_axis]] + spot[main_axis + 1:]
    return result.at[tuple(spot)].set(smallest).at[tuple(next_to)].set(high)


def block_scale(key, dims, cuts, low, high):
    def one(dim, parts):
        heights = jax.random.uniform(jax.random.fold_in(jax.random.fold_in(key, 6), dim), (parts,), jnp.float32, low / len(cuts), high / len(cuts))
        return jnp.repeat(jnp.exp(heights), dims[dim] // parts).reshape((-1,) + (1,) * (len(dims) - dim - 1))

    level = one(*cuts[0])
    for cut in cuts[1:]:
        level = level * one(*cut)
    return level


def normal_values(rng, dims, scale, most, cuts=(), kind=jnp.bfloat16):
    result = jax.random.normal(rng, dims, jnp.float32) * scale
    if len(cuts) > 0:
        result = block_scale(rng, dims, cuts, -0.22, 0.18) * result
    return jnp.clip(result, min=-most, max=most).astype(kind)


def setup_inputs(seed: int = 0) -> dict:
    seeds = jax.random.split(jax.random.key(seed), 7)
    text_hidden = normal_values(seeds[0], (SAMPLES, TXT, D), 1.0, 6.0, ((0, 16), (1, 16), (2, 2)))
    text_qkv_weight = normal_values(seeds[1], (D, HEADS, 3 * HS), D ** -0.5, 0.109375, ((0, 2), (1, 16)))
    image_qkv = draw_image_qkv(jax.random.fold_in(seeds[6], 71), 0)
    mod_weight = normal_values(seeds[3], (FREQ, HEADS, HS), FREQ ** -0.5, 0.375, ((1, 16),), jnp.float32)
    lengths = draw_lengths(jax.random.fold_in(seeds[6], 71), 0)
    timesteps = place_ends(jax.random.randint(seeds[5], (SAMPLES,), 0, 1000), jax.random.fold_in(seeds[5], 1), 0, 999).astype(jnp.int32)
    return dict(text_hidden=text_hidden, text_qkv_weight=text_qkv_weight, image_qkv=image_qkv, mod_weight=mod_weight, lengths=lengths, timesteps=timesteps)


def pick_block(row_count):
    if row_count <= 1024:
        return row_count
    options = [size for size in range(512, row_count + 1) if row_count % size == 0]
    return options[0]

def gate_of(timestep, mod_weight):
    width = mod_weight.shape[0]
    half_width = width // 2
    frequency = jnp.exp(-math.log(10000.0) * jnp.arange(half_width, dtype=jnp.float32) / half_width)
    angles = timestep.astype(jnp.float32) * frequency
    embedding = jnp.concatenate([jnp.cos(angles), jnp.sin(angles)])
    flat = mod_weight.reshape(width, -1)
    gate_scale = jnp.dot(embedding[None, :], flat, precision=lax.Precision.HIGHEST)
    return gate_scale.reshape(mod_weight.shape[1], mod_weight.shape[2])

def attend(joint, length, text_rows, gate_scale):
    row_count = joint.shape[0]
    head_count = joint.shape[1]
    head_size = gate_scale.shape[1]
    queries = joint[:, :, :head_size]
    key_rows = joint[:, :, head_size:2 * head_size]
    value_rows = joint[:, :, 2 * head_size:]
    block_rows = pick_block(row_count)
    position = jnp.arange(row_count)
    key_valid = (position >= text_rows) | (position < length)
    score_scale = 1.0 / math.sqrt(head_size)
    query_blocks = queries.reshape(row_count // block_rows, block_rows, head_count, head_size)

    def one_block(query_block):
        scores = jnp.einsum('qhc,khc->hqk', query_block, key_rows, preferred_element_type=jnp.float32) * score_scale
        scores = jnp.where(key_valid[None, None, :], scores, -jnp.inf)
        largest = lax.optimization_barrier(jnp.max(scores, axis=-1, keepdims=True))
        expo = jnp.exp(scores - largest)
        weights = (expo / lax.optimization_barrier(jnp.sum(expo, axis=-1, keepdims=True))).astype(jnp.bfloat16)
        output = jnp.einsum('hqk,khc->qhc', weights, value_rows, preferred_element_type=jnp.float32)
        return (output * gate_scale[None, :, :]).astype(jnp.bfloat16)
    return lax.map(one_block, query_blocks).reshape(row_count, head_count, head_size)

def reference(text_hidden, text_qkv_weight, image_qkv, mod_weight, lengths, timesteps):
    groups = text_hidden.reshape(N_SEC, N_TP, TXT, D)
    groups = jnp.roll(groups, -(N_SEC // 2), axis=0).reshape(SAMPLES, TXT, D)

    def one_sample(inputs):
        text_rows, image_rows, length, timestep = inputs
        text_qkv = jnp.einsum('rd,dhc->rhc', text_rows, text_qkv_weight, preferred_element_type=jnp.float32).astype(jnp.bfloat16)
        joint = jnp.concatenate([text_qkv, image_rows], axis=0)
        gate_scale = gate_of(timestep, mod_weight)
        return attend(joint, length, TXT, gate_scale)
    attended = lax.map(one_sample, (groups, image_qkv, lengths, timesteps))
    return (attended[:, TXT:], attended[:, :TXT])
```

```python
import functools
import math

import jax
import jax.numpy as jnp
from jax import lax
from jax.experimental import pallas as pl
from jax.experimental.pallas import tpu as pltpu
from jax.sharding import PartitionSpec as P

TRANSPOSED = (((1,), (1,)), ((), ()))


def gate_of(timestep, mod_weight):
    width = mod_weight.shape[0]
    half_width = width // 2
    frequency = jnp.exp(-math.log(10000.0) * jnp.arange(half_width, dtype=jnp.float32) / half_width)
    angles = timestep.astype(jnp.float32) * frequency
    embedding = jnp.concatenate([jnp.cos(angles), jnp.sin(angles)])
    flat = mod_weight.reshape(width, -1)
    return jnp.dot(embedding[None, :], flat, precision=lax.Precision.HIGHEST)


def attend_kernel(length_ref, image_ref, text_ref, gate_ref, image_out, text_out, *, rows, unroll):
    head = gate_ref.shape[1]
    text_count = text_ref.shape[0]
    block_count = image_ref.shape[0] // (rows * unroll)
    scale = math.log2(math.e) / math.sqrt(head)
    text_keys = text_ref[:, head : 2 * head]
    image_keys = image_ref[:, head : 2 * head]
    text_values = text_ref[:, 2 * head :]
    text_values = jnp.concatenate([text_values, jnp.ones_like(text_values)], axis=1)
    image_values = image_ref[:, 2 * head :]
    image_values = jnp.concatenate([image_values, jnp.ones_like(image_values)], axis=1)
    gate = gate_ref[...]
    position = lax.broadcasted_iota(jnp.int32, (1, text_count), 1)
    excluded = jnp.where(position < length_ref[0], 0.0, -jnp.inf)

    def one_block(queries):
        text_scores = lax.dot_general(
            queries, text_keys, TRANSPOSED, preferred_element_type=jnp.float32
        )
        text_scores = text_scores + excluded
        image_scores = lax.dot_general(
            queries, image_keys, TRANSPOSED, preferred_element_type=jnp.float32
        )
        largest = jnp.maximum(
            jnp.max(text_scores, axis=-1, keepdims=True),
            jnp.max(image_scores, axis=-1, keepdims=True),
        )
        text_weights = jnp.exp2((text_scores - largest) * scale).astype(jnp.bfloat16)
        image_weights = jnp.exp2((image_scores - largest) * scale).astype(jnp.bfloat16)
        total = jnp.dot(text_weights, text_values, preferred_element_type=jnp.float32)
        total = total + jnp.dot(image_weights, image_values, preferred_element_type=jnp.float32)
        return (total[:, :head] * (gate / total[:, head:])).astype(jnp.bfloat16)

    step = pl.program_id(0)

    @pl.when(step < block_count)
    def _():
        for part in range(unroll):
            at = pl.ds(pl.multiple_of((step * unroll + part) * rows, rows), rows)
            image_out[at, :] = one_block(image_ref[at, :head])

    @pl.when(step == block_count)
    def _():
        text_out[...] = one_block(text_ref[:, :head])


def attend(image, text, length, gate_scale):
    image_count, width = image.shape
    text_count = text.shape[0]
    head = width // 3
    rows, unroll = 512, 2
    whole = lambda shape: pl.BlockSpec(shape, lambda i: (0, 0))
    return pl.pallas_call(
        functools.partial(attend_kernel, rows=rows, unroll=unroll),
        grid=(image_count // (rows * unroll) + 1,),
        in_specs=[
            pl.BlockSpec(memory_space=pltpu.SMEM),
            whole((image_count, width)),
            whole((text_count, width)),
            whole((1, head)),
        ],
        out_specs=[whole((image_count, head)), whole((text_count, head))],
        out_shape=[
            jax.ShapeDtypeStruct((image_count, head), jnp.bfloat16),
            jax.ShapeDtypeStruct((text_count, head), jnp.bfloat16),
        ],
        compiler_params=pltpu.CompilerParams(vmem_limit_bytes=48 * 2**20),
    )(length, image, text, gate_scale)


def shards(text_hidden, text_qkv_weight, image_qkv, mod_weight, lengths, timesteps):
    sec, sp, tp = (lax.axis_size(axis) for axis in ("sec", "sp", "tp"))
    mine = lax.axis_index("tp")
    other = 1 - mine

    def to_group(x, flip):
        moves = [
            (s * tp + t, ((s + sec // 2) % sec) * tp + (t + flip) % tp)
            for s in range(sec)
            for t in range(tp)
        ]
        return lax.ppermute(x, ("sec", "tp"), moves)

    near = to_group(lax.dynamic_index_in_dim(text_hidden, mine, 0, keepdims=False), 0)
    far = to_group(lax.dynamic_index_in_dim(text_hidden, other, 0, keepdims=False), 1)
    halves = lax.all_gather(jnp.stack([near, far]), "sp", axis=1, tiled=True)
    own_weight = text_qkv_weight[:, 0]
    other_weight = lax.ppermute(own_weight, "tp", [(0, 1), (1, 0)])

    by_head = image_qkv[0].transpose(1, 0, 2)
    image = lax.all_to_all(by_head, "sp", split_axis=0, concat_axis=0)
    heads, rows, width = image.shape
    gate_scale = gate_of(timesteps[0], mod_weight)

    text = jnp.dot(halves[0], own_weight, preferred_element_type=jnp.float32)
    text = text + jnp.dot(halves[1], other_weight, preferred_element_type=jnp.float32)
    image_heads, text_out = attend(
        image.reshape(heads * rows, width), text.astype(jnp.bfloat16), lengths, gate_scale
    )
    image_out = lax.all_to_all(
        image_heads.reshape(sp, rows, width // 3), "sp", split_axis=0, concat_axis=0
    )
    return (image_out.transpose(1, 0, 2)[None], text_out[None, :, None, :])


def solution(mesh):
    in_specs = (
        P("sec", "sp", "tp"),
        P("tp", "sp", None),
        P(("sec", "tp"), "sp", None, None),
        P(None, "sp", None),
        P(("sec", "tp")),
        P(("sec", "tp")),
    )
    out_specs = (P(("sec", "tp"), "sp", None, None), P(("sec", "tp"), None, "sp", None))
    return jax.shard_map(shards, mesh=mesh, in_specs=in_specs, out_specs=out_specs, check_vma=False)
```

```python
import functools
import math

import jax
import jax.numpy as jnp
from jax import lax
from jax.experimental import pallas as pl
from jax.experimental.pallas import tpu as pltpu
from jax.sharding import PartitionSpec as P

TRANSPOSED = (((1,), (1,)), ((), ()))


def gate_of(timestep, mod_weight):
    width = mod_weight.shape[0]
    half_width = width // 2
    frequency = jnp.exp(-math.log(10000.0) * jnp.arange(half_width, dtype=jnp.float32) / half_width)
    angles = timestep.astype(jnp.float32) * frequency
    embedding = jnp.concatenate([jnp.cos(angles), jnp.sin(angles)])
    flat = mod_weight.reshape(width, -1)
    return jnp.dot(embedding[None, :], flat, precision=lax.Precision.HIGHEST)


def collect_kernel(own, up, across, down, quad, upper, lower):
    for place, block in enumerate((own, up, across, down)):
        quad[place] = block[...]
    upper[0] = own[...]
    upper[1] = up[...]
    lower[0] = down[...]
    lower[1] = own[...]


def collect(own, up, across, down):
    vmem = pl.BlockSpec(memory_space=pltpu.VMEM)
    shape = lambda count: jax.ShapeDtypeStruct((count,) + own.shape, own.dtype)
    return pl.pallas_call(
        collect_kernel,
        in_specs=[vmem] * 4,
        out_specs=[vmem] * 3,
        out_shape=[shape(4), shape(2), shape(2)],
        compiler_params=pltpu.CompilerParams(vmem_limit_bytes=16 * 2**20),
        cost_estimate=pl.CostEstimate(flops=10**11, bytes_accessed=8 * own.size, transcendentals=0),
    )(own, up, across, down)


def project_kernel(
    places_ref, quad, after, upper, lower, behind, weight_ref, near_ref, far_ref, rows_ref
):
    mine = places_ref[0]
    turn = places_ref[1]
    size = quad.shape[2]
    pieces = rows_ref.shape[0] // size
    weight = weight_ref[...]
    parts = [(quad, place, 4 * place) for place in range(4)]
    parts += [(after, place, 4 * place + 1) for place in range(4)]
    parts += [(upper, place, 4 * place + 2) for place in range(2)]
    parts += [(lower, place, 4 * place + 10) for place in range(2)]
    parts += [(behind, place, (4 * place + 15) % 16) for place in range(4)]
    for sample, out in ((1 - mine, far_ref), (mine, near_ref)):
        for part, place, offset in parts:
            at = pl.ds(pl.multiple_of(lax.rem(turn + offset, pieces) * size, size), size)
            rows_ref[at, :] = part[place, sample]
        out[...] = jnp.dot(rows_ref[...], weight, preferred_element_type=jnp.float32)


def project(places, parts, weight, sp):
    rows = sp * parts[0].shape[2]
    vmem = pl.BlockSpec(memory_space=pltpu.VMEM)
    return pl.pallas_call(
        project_kernel,
        in_specs=[pl.BlockSpec(memory_space=pltpu.SMEM)] + [vmem] * 6,
        out_specs=[vmem, vmem],
        out_shape=[jax.ShapeDtypeStruct((rows, weight.shape[1]), jnp.float32)] * 2,
        scratch_shapes=[pltpu.VMEM((rows, weight.shape[0]), jnp.bfloat16)],
        compiler_params=pltpu.CompilerParams(vmem_limit_bytes=24 * 2**20),
        cost_estimate=pl.CostEstimate(flops=10**11, bytes_accessed=2 * weight.size, transcendentals=0),
    )(places, *parts, weight)


def attend_kernel(
    length_ref, queries_ref, pairs_ref, near_ref, far_ref, gate_ref, image_out, text_out,
    keys_ref, values_ref, *, rows
):
    head = gate_ref.shape[1]
    text_count = near_ref.shape[0]
    scale = math.log2(math.e) / math.sqrt(head)
    text = (near_ref[...] + far_ref[...]).astype(jnp.bfloat16)
    keys_ref[:text_count, :] = text[:, head : 2 * head]
    keys_ref[text_count:, :] = pairs_ref[:, :head]
    values_ref[:text_count, :head] = text[:, 2 * head :]
    values_ref[text_count:, :head] = pairs_ref[:, head:]
    values_ref[:, head:] = jnp.ones((values_ref.shape[0], head), jnp.bfloat16)
    gate = gate_ref[...]
    position = lax.broadcasted_iota(jnp.int32, (1, text_count), 1)
    excluded = jnp.where(position < length_ref[0], 0.0, -jnp.inf)

    def one_block(queries):
        scores = lax.dot_general(
            queries, keys_ref[...], TRANSPOSED, preferred_element_type=jnp.float32
        )
        scores = jnp.concatenate(
            [scores[:, :text_count] + excluded, scores[:, text_count:]], axis=1
        )
        largest = jnp.max(scores, axis=-1, keepdims=True)
        weights = jnp.exp2((scores - largest) * scale).astype(jnp.bfloat16)
        total = jnp.dot(weights, values_ref[...], preferred_element_type=jnp.float32)
        return (total[:, :head] * (gate / total[:, head:])).astype(jnp.bfloat16)

    for block in range(queries_ref.shape[0] // rows):
        at = pl.ds(block * rows, rows)
        image_out[at, :] = one_block(queries_ref[at, :])
    text_out[...] = one_block(text[:, :head])


def attend(queries, pairs, near, far, length, gate_scale):
    image_count, head = queries.shape
    text_count = near.shape[0]
    keys = text_count + image_count
    vmem = pl.BlockSpec(memory_space=pltpu.VMEM)
    return pl.pallas_call(
        functools.partial(attend_kernel, rows=512),
        in_specs=[pl.BlockSpec(memory_space=pltpu.SMEM)] + [vmem] * 5,
        out_specs=[vmem, vmem],
        out_shape=[
            jax.ShapeDtypeStruct((image_count, head), jnp.bfloat16),
            jax.ShapeDtypeStruct((text_count, head), jnp.bfloat16),
        ],
        scratch_shapes=[
            pltpu.VMEM((keys, head), jnp.bfloat16),
            pltpu.VMEM((keys, 2 * head), jnp.bfloat16),
        ],
        compiler_params=pltpu.CompilerParams(vmem_limit_bytes=48 * 2**20),
    )(length, queries, pairs, near, far, gate_scale)


def shards(text_hidden, text_qkv_weight, image_qkv, mod_weight, lengths, timesteps):
    sec, sp, tp = (lax.axis_size(axis) for axis in ("sec", "sp", "tp"))
    mine = lax.axis_index("tp")
    head = mod_weight.shape[2]

    def ahead(x, by):
        return lax.ppermute(x, "sp", [((i + by) % sp, i) for i in range(sp)])

    def to_group(x, flip):
        moves = [
            (s * tp + t, ((s + sec // 2) % sec) * tp + (t + flip) % tp)
            for s in range(sec)
            for t in range(tp)
        ]
        return lax.ppermute(x, ("sec", "tp"), moves)

    across = ahead(text_hidden, 8)
    up = ahead(text_hidden, 4)
    down = ahead(text_hidden, -4)
    queries = image_qkv[0, :, :, :head].transpose(1, 0, 2)
    pairs = image_qkv[0, :, :, head:].transpose(1, 0, 2)
    queries = lax.all_to_all(queries, "sp", split_axis=0, concat_axis=0)
    heads, rows, _ = queries.shape
    gate_scale = gate_of(timesteps[0], mod_weight)

    quad, upper, lower = collect(text_hidden, up, across, down)
    after = ahead(quad, 1)
    behind = ahead(quad, -1)
    upper = ahead(upper, 2)
    lower = ahead(lower, -2)

    pairs, queries = lax.optimization_barrier((pairs, queries))
    pairs = lax.all_to_all(pairs, "sp", split_axis=0, concat_axis=0)

    places = jnp.stack([mine, lax.axis_index("sp")]).astype(jnp.int32)
    near, far = project(
        places, (quad, after, upper, lower, behind), text_qkv_weight[:, 0], sp
    )
    near = to_group(near, 0)
    far = to_group(far, 1)

    image_heads, text_out = attend(
        queries.reshape(heads * rows, head),
        pairs.reshape(heads * rows, 2 * head),
        near,
        far,
        lengths,
        gate_scale,
    )
    image_out = lax.all_to_all(
        image_heads.reshape(sp, rows, head), "sp", split_axis=0, concat_axis=0
    )
    return (image_out.transpose(1, 0, 2)[None], text_out[None, :, None, :])


def solution(mesh):
    in_specs = (
        P("sec", "sp", "tp"),
        P("tp", "sp", None),
        P(("sec", "tp"), "sp", None, None),
        P(None, "sp", None),
        P(("sec", "tp")),
        P(("sec", "tp")),
    )
    out_specs = (P(("sec", "tp"), "sp", None, None), P(("sec", "tp"), None, "sp", None))
    return jax.shard_map(shards, mesh=mesh, in_specs=in_specs, out_specs=out_specs, check_vma=False)
```

```python
import functools
import math

import jax
import jax.numpy as jnp
from jax import lax
from jax.experimental import pallas as pl
from jax.experimental.pallas import tpu as pltpu
from jax.sharding import PartitionSpec as P

TRANSPOSED = (((1,), (1,)), ((), ()))


def gate_of(timestep, mod_weight):
    width = mod_weight.shape[0]
    half_width = width // 2
    frequency = jnp.exp(-math.log(10000.0) * jnp.arange(half_width, dtype=jnp.float32) / half_width)
    angles = timestep.astype(jnp.float32) * frequency
    embedding = jnp.concatenate([jnp.cos(angles), jnp.sin(angles)])
    flat = mod_weight.reshape(width, -1)
    return jnp.dot(embedding[None, :], flat, precision=lax.Precision.HIGHEST)


def collect_kernel(own, up, across, down, quad, upper, lower):
    for place, block in enumerate((own, up, across, down)):
        quad[place] = block[...]
    upper[0] = own[...]
    upper[1] = up[...]
    lower[0] = down[...]
    lower[1] = own[...]


def collect(own, up, across, down):
    vmem = pl.BlockSpec(memory_space=pltpu.VMEM)
    shape = lambda count: jax.ShapeDtypeStruct((count,) + own.shape, own.dtype)
    return pl.pallas_call(
        collect_kernel,
        in_specs=[vmem] * 4,
        out_specs=[vmem] * 3,
        out_shape=[shape(4), shape(2), shape(2)],
        compiler_params=pltpu.CompilerParams(vmem_limit_bytes=16 * 2**20),
        cost_estimate=pl.CostEstimate(flops=10**11, bytes_accessed=8 * own.size, transcendentals=0),
    )(own, up, across, down)


def project_kernel(
    turn_ref, quad, after, upper, lower, behind, own_weight, other_weight, out_ref, rows_ref
):
    size = quad.shape[1]
    half = own_weight.shape[0]
    pieces = rows_ref.shape[0] // size
    parts = [(quad, place, 4 * place) for place in range(4)]
    parts += [(after, place, 4 * place + 1) for place in range(4)]
    parts += [(upper, place, 4 * place + 2) for place in range(2)]
    parts += [(lower, place, 4 * place + 10) for place in range(2)]
    parts += [(behind, place, (4 * place + 15) % 16) for place in range(4)]
    for part, place, offset in parts:
        at = pl.ds(pl.multiple_of(lax.rem(turn_ref[0] + offset, pieces) * size, size), size)
        rows_ref[at, :] = part[place]
    total = jnp.dot(rows_ref[:, :half], own_weight[...], preferred_element_type=jnp.float32)
    total = total + jnp.dot(
        rows_ref[:, half:], other_weight[...], preferred_element_type=jnp.float32
    )
    out_ref[...] = total.astype(out_ref.dtype)


def project(turn, parts, own_weight, other_weight, sp):
    rows = sp * parts[0].shape[1]
    vmem = pl.BlockSpec(memory_space=pltpu.VMEM)
    return pl.pallas_call(
        project_kernel,
        in_specs=[pl.BlockSpec(memory_space=pltpu.SMEM)] + [vmem] * 7,
        out_specs=vmem,
        out_shape=jax.ShapeDtypeStruct((rows, own_weight.shape[1]), jnp.bfloat16),
        scratch_shapes=[pltpu.VMEM((rows, 2 * own_weight.shape[0]), jnp.bfloat16)],
        compiler_params=pltpu.CompilerParams(vmem_limit_bytes=24 * 2**20),
        cost_estimate=pl.CostEstimate(flops=10**11, bytes_accessed=10**6, transcendentals=0),
    )(turn, *parts, own_weight, other_weight)


def attender(length_ref, image_values, mixed_ref, text_ref, gate_ref, keys_ref, values_ref):
    text_count, width = text_ref.shape
    head = width // 3
    lines, rows, _ = image_values.shape
    scale = math.log2(math.e) / math.sqrt(head)
    keys_ref[:text_count, :] = text_ref[:, head : 2 * head]
    keys_ref[text_count:, :] = mixed_ref[:, :rows, :].reshape(lines * rows, head)
    values_ref[:text_count, :head] = text_ref[:, 2 * head :]
    values_ref[text_count:, :head] = image_values[...].reshape(lines * rows, head)
    values_ref[:, head:] = jnp.ones((values_ref.shape[0], head), jnp.bfloat16)
    gate = gate_ref[...]
    position = lax.broadcasted_iota(jnp.int32, (1, text_count), 1)
    excluded = jnp.where(position < length_ref[0], 0.0, -jnp.inf)

    def one_block(queries):
        scores = lax.dot_general(
            queries, keys_ref[...], TRANSPOSED, preferred_element_type=jnp.float32
        )
        scores = jnp.concatenate(
            [scores[:, :text_count] + excluded, scores[:, text_count:]], axis=1
        )
        largest = jnp.max(scores, axis=-1, keepdims=True)
        weights = jnp.exp2((scores - largest) * scale).astype(jnp.bfloat16)
        total = jnp.dot(weights, values_ref[...], preferred_element_type=jnp.float32)
        return (total[:, :head] * (gate / total[:, head:])).astype(jnp.bfloat16)

    return one_block


def early_kernel(
    length_ref, image_values, mixed_ref, text_ref, gate_ref, early_out, text_out, keys_ref, values_ref
):
    one_block = attender(
        length_ref, image_values, mixed_ref, text_ref, gate_ref, keys_ref, values_ref
    )
    lines, rows, head = early_out.shape
    first = mixed_ref.shape[1] - rows
    for line in range(0, lines, 8):
        queries = mixed_ref[line : line + 8, first:, :].reshape(8 * rows, head)
        early_out[line : line + 8] = one_block(queries).reshape(8, rows, head)
    text_out[...] = one_block(text_ref[:, :head])


def late_kernel(
    length_ref, image_values, mixed_ref, text_ref, gate_ref, late_ref, early_ref, image_out,
    keys_ref, values_ref
):
    one_block = attender(
        length_ref, image_values, mixed_ref, text_ref, gate_ref, keys_ref, values_ref
    )
    lines, rows, head = late_ref.shape
    half = early_ref.shape[1]
    image_out[:, :half, :] = early_ref[...]
    for line in range(0, lines, 8):
        queries = late_ref[line : line + 8].reshape(8 * rows, head)
        image_out[line : line + 8, half:, :] = one_block(queries).reshape(8, rows, head)


def attend(kernel, outs, length, values, mixed, text, gate_scale, *more):
    lines, rows, head = values.shape
    count = text.shape[0] + lines * rows
    vmem = pl.BlockSpec(memory_space=pltpu.VMEM)
    return pl.pallas_call(
        kernel,
        in_specs=[pl.BlockSpec(memory_space=pltpu.SMEM)] + [vmem] * (4 + len(more)),
        out_specs=[vmem] * len(outs),
        out_shape=[jax.ShapeDtypeStruct(shape, jnp.bfloat16) for shape in outs],
        scratch_shapes=[
            pltpu.VMEM((count, head), jnp.bfloat16),
            pltpu.VMEM((count, 2 * head), jnp.bfloat16),
        ],
        compiler_params=pltpu.CompilerParams(vmem_limit_bytes=40 * 2**20),
        cost_estimate=pl.CostEstimate(flops=10**9, bytes_accessed=10**6, transcendentals=0),
    )(length, values, mixed, text, gate_scale, *more)


def shards(text_hidden, text_qkv_weight, image_qkv, mod_weight, lengths, timesteps):
    sec, sp, tp = (lax.axis_size(axis) for axis in ("sec", "sp", "tp"))
    mine = lax.axis_index("tp")
    head = mod_weight.shape[2]

    def ahead(x, by):
        return lax.ppermute(x, "sp", [((i + by) % sp, i) for i in range(sp)])

    def to_group(x, flip):
        moves = [
            (s * tp + t, ((s + sec // 2) % sec) * tp + (t + flip) % tp)
            for s in range(sec)
            for t in range(tp)
        ]
        return lax.ppermute(x, ("sec", "tp"), moves)

    def to_heads(x):
        return lax.all_to_all(x, "sp", split_axis=0, concat_axis=0)

    half = image_qkv.shape[1] // 2
    keys = image_qkv[0, :, :, head : 2 * head].transpose(1, 0, 2)
    values = image_qkv[0, :, :, 2 * head :].transpose(1, 0, 2)
    early = image_qkv[0, :half, :, :head].transpose(1, 0, 2)
    late = image_qkv[0, half:, :, :head].transpose(1, 0, 2)
    mixed = to_heads(jnp.concatenate([keys, early], axis=1))

    near = to_group(lax.dynamic_index_in_dim(text_hidden, mine, 0, keepdims=False), 0)
    far = to_group(lax.dynamic_index_in_dim(text_hidden, 1 - mine, 0, keepdims=False), 1)
    own = jnp.concatenate([near, far], axis=1)
    own_weight = text_qkv_weight[:, 0]
    across = ahead(own, 8)
    up = ahead(own, 4)
    down = ahead(own, -4)
    values, mixed = lax.optimization_barrier((values, mixed))
    values = to_heads(values)
    gate_scale = gate_of(timesteps[0], mod_weight)

    quad, upper, lower = collect(own, up, across, down)
    after = ahead(quad, 1)
    behind = ahead(quad, -1)
    upper = ahead(upper, 2)
    lower = ahead(lower, -2)
    sent, quad = lax.optimization_barrier((own_weight, quad))
    other_weight = lax.ppermute(sent, "tp", [(0, 1), (1, 0)])
    late, values = lax.optimization_barrier((late, values))
    late = to_heads(late)

    turn = lax.axis_index("sp").astype(jnp.int32).reshape(1)
    text = project(turn, (quad, after, upper, lower, behind), own_weight, other_weight, sp)
    part = (sp, half, head)
    early, text_out = attend(
        early_kernel, (part, (text.shape[0], head)), lengths, values, mixed, text, gate_scale
    )
    (image_heads,) = attend(
        late_kernel, ((sp, 2 * half, head),), lengths, values, mixed, text, gate_scale, late, early
    )
    image_out = to_heads(image_heads)
    return (image_out.transpose(1, 0, 2)[None], text_out[None, :, None, :])


def solution(mesh):
    in_specs = (
        P("sec", "sp", "tp"),
        P("tp", "sp", None),
        P(("sec", "tp"), "sp", None, None),
        P(None, "sp", None),
        P(("sec", "tp")),
        P(("sec", "tp")),
    )
    out_specs = (P(("sec", "tp"), "sp", None, None), P(("sec", "tp"), None, "sp", None))
    return jax.shard_map(shards, mesh=mesh, in_specs=in_specs, out_specs=out_specs, check_vma=False)
```

```python
import functools
import math

import jax
import jax.numpy as jnp
from jax import lax
from jax.experimental import pallas as pl
from jax.experimental.pallas import tpu as pltpu
from jax.sharding import PartitionSpec as P

TRANSPOSED = (((1,), (1,)), ((), ()))


def gate_of(timestep, mod_weight):
    width = mod_weight.shape[0]
    half_width = width // 2
    frequency = jnp.exp(-math.log(10000.0) * jnp.arange(half_width, dtype=jnp.float32) / half_width)
    angles = timestep.astype(jnp.float32) * frequency
    embedding = jnp.concatenate([jnp.cos(angles), jnp.sin(angles)])
    flat = mod_weight.reshape(width, -1)
    return jnp.dot(embedding[None, :], flat, precision=lax.Precision.HIGHEST)


def collect_kernel(own, up, across, down, quad):
    for place, block in enumerate((own, up, across, down)):
        quad[place] = block[...]


def collect(own, up, across, down):
    vmem = pl.BlockSpec(memory_space=pltpu.VMEM)
    return pl.pallas_call(
        collect_kernel,
        in_specs=[vmem] * 4,
        out_specs=vmem,
        out_shape=jax.ShapeDtypeStruct((4,) + own.shape, own.dtype),
        compiler_params=pltpu.CompilerParams(vmem_limit_bytes=16 * 2**20),
        cost_estimate=pl.CostEstimate(flops=10**11, bytes_accessed=10**6, transcendentals=0),
    )(own, up, across, down)


def project_kernel(
    turn_ref, quad, after, middle, behind, own_weight, other_weight, out_ref, rows_ref
):
    size = quad.shape[1]
    half = own_weight.shape[0]
    pieces = rows_ref.shape[0] // size
    parts = [(quad, place, 4 * place) for place in range(4)]
    parts += [(after, place, 4 * place + 1) for place in range(4)]
    parts += [(middle, place, 4 * place + turn_ref[1]) for place in range(4)]
    parts += [(behind, place, (4 * place + 15) % 16) for place in range(4)]
    for part, place, offset in parts:
        at = pl.ds(pl.multiple_of(lax.rem(turn_ref[0] + offset, pieces) * size, size), size)
        rows_ref[at, :] = part[place]
    total = jnp.dot(rows_ref[:, :half], own_weight[...], preferred_element_type=jnp.float32)
    total = total + jnp.dot(
        rows_ref[:, half:], other_weight[...], preferred_element_type=jnp.float32
    )
    out_ref[...] = total.astype(out_ref.dtype)


def project(turn, parts, own_weight, other_weight, sp):
    rows = sp * parts[0].shape[1]
    vmem = pl.BlockSpec(memory_space=pltpu.VMEM)
    return pl.pallas_call(
        project_kernel,
        in_specs=[pl.BlockSpec(memory_space=pltpu.SMEM)] + [vmem] * 6,
        out_specs=vmem,
        out_shape=jax.ShapeDtypeStruct((rows, own_weight.shape[1]), jnp.bfloat16),
        scratch_shapes=[pltpu.VMEM((rows, 2 * own_weight.shape[0]), jnp.bfloat16)],
        compiler_params=pltpu.CompilerParams(vmem_limit_bytes=24 * 2**20),
        cost_estimate=pl.CostEstimate(flops=10**11, bytes_accessed=10**6, transcendentals=0),
    )(turn, *parts, own_weight, other_weight)


def attender(length_ref, image_values, mixed_ref, text_ref, gate_ref, keys_ref, values_ref):
    text_count, width = text_ref.shape
    head = width // 3
    lines, rows, _ = image_values.shape
    scale = math.log2(math.e) / math.sqrt(head)
    keys_ref[:text_count, :] = text_ref[:, head : 2 * head]
    keys_ref[text_count:, :] = mixed_ref[:, :rows, :].reshape(lines * rows, head)
    values_ref[:text_count, :head] = text_ref[:, 2 * head :]
    values_ref[text_count:, :head] = image_values[...].reshape(lines * rows, head)
    values_ref[:, head:] = jnp.ones((values_ref.shape[0], head), jnp.bfloat16)
    gate = gate_ref[...]
    position = lax.broadcasted_iota(jnp.int32, (1, text_count), 1)
    excluded = jnp.where(position < length_ref[0], 0.0, -jnp.inf)

    def one_block(queries):
        scores = lax.dot_general(
            queries, keys_ref[...], TRANSPOSED, preferred_element_type=jnp.float32
        )
        scores = jnp.concatenate(
            [scores[:, :text_count] + excluded, scores[:, text_count:]], axis=1
        )
        largest = jnp.max(scores, axis=-1, keepdims=True)
        weights = jnp.exp2((scores - largest) * scale).astype(jnp.bfloat16)
        total = jnp.dot(weights, values_ref[...], preferred_element_type=jnp.float32)
        return (total[:, :head] * (gate / total[:, head:])).astype(jnp.bfloat16)

    return one_block


def early_kernel(
    length_ref, image_values, mixed_ref, text_ref, gate_ref, early_out, text_out, keys_ref, values_ref
):
    one_block = attender(
        length_ref, image_values, mixed_ref, text_ref, gate_ref, keys_ref, values_ref
    )
    lines, rows, head = early_out.shape
    first = mixed_ref.shape[1] - rows
    for line in range(0, lines, 8):
        queries = mixed_ref[line : line + 8, first:, :].reshape(8 * rows, head)
        early_out[line : line + 8] = one_block(queries).reshape(8, rows, head)
    text_out[...] = one_block(text_ref[:, :head])


def late_kernel(
    length_ref, image_values, mixed_ref, text_ref, gate_ref, late_ref, early_ref, image_out,
    keys_ref, values_ref
):
    one_block = attender(
        length_ref, image_values, mixed_ref, text_ref, gate_ref, keys_ref, values_ref
    )
    lines, rows, head = late_ref.shape
    half = early_ref.shape[1]
    image_out[:, :half, :] = early_ref[...]
    for line in range(0, lines, 8):
        queries = late_ref[line : line + 8].reshape(8 * rows, head)
        image_out[line : line + 8, half:, :] = one_block(queries).reshape(8, rows, head)


def attend(kernel, outs, length, values, mixed, text, gate_scale, *more):
    lines, rows, head = values.shape
    count = text.shape[0] + lines * rows
    vmem = pl.BlockSpec(memory_space=pltpu.VMEM)
    return pl.pallas_call(
        kernel,
        in_specs=[pl.BlockSpec(memory_space=pltpu.SMEM)] + [vmem] * (4 + len(more)),
        out_specs=[vmem] * len(outs),
        out_shape=[jax.ShapeDtypeStruct(shape, jnp.bfloat16) for shape in outs],
        scratch_shapes=[
            pltpu.VMEM((count, head), jnp.bfloat16),
            pltpu.VMEM((count, 2 * head), jnp.bfloat16),
        ],
        compiler_params=pltpu.CompilerParams(vmem_limit_bytes=40 * 2**20),
        cost_estimate=pl.CostEstimate(flops=10**9, bytes_accessed=10**6, transcendentals=0),
    )(length, values, mixed, text, gate_scale, *more)


def shards(text_hidden, text_qkv_weight, image_qkv, mod_weight, lengths, timesteps):
    sec, sp, tp = (lax.axis_size(axis) for axis in ("sec", "sp", "tp"))
    mine = lax.axis_index("tp")
    head = mod_weight.shape[2]

    def ahead(x, by):
        return lax.ppermute(x, "sp", [((i + by) % sp, i) for i in range(sp)])

    def to_group(x, flip):
        moves = [
            (s * tp + t, ((s + sec // 2) % sec) * tp + (t + flip) % tp)
            for s in range(sec)
            for t in range(tp)
        ]
        return lax.ppermute(x, ("sec", "tp"), moves)

    def to_heads(x):
        return lax.all_to_all(x, "sp", split_axis=0, concat_axis=0)

    half = image_qkv.shape[1] // 2
    keys = image_qkv[0, :, :, head : 2 * head].transpose(1, 0, 2)
    values = image_qkv[0, :, :, 2 * head :].transpose(1, 0, 2)
    early = image_qkv[0, :half, :, :head].transpose(1, 0, 2)
    late = image_qkv[0, half:, :, :head].transpose(1, 0, 2)
    mixed = to_heads(jnp.concatenate([keys, early], axis=1))

    near = to_group(lax.dynamic_index_in_dim(text_hidden, mine, 0, keepdims=False), 0)
    far = to_group(lax.dynamic_index_in_dim(text_hidden, 1 - mine, 0, keepdims=False), 1)
    own = jnp.concatenate([near, far], axis=1)
    own_weight = text_qkv_weight[:, 0]
    across = ahead(own, 8)
    up = ahead(own, 4)
    down = ahead(own, -4)
    values, mixed = lax.optimization_barrier((values, mixed))
    values = to_heads(values)
    gate_scale = gate_of(timesteps[0], mod_weight)

    quad = collect(own, up, across, down)
    after = ahead(quad, 1)
    behind = ahead(quad, -1)
    apart = [2 if s % 2 == 0 else -2 for s in range(sec)]
    moves = [(s * sp + (i + apart[s]) % sp, s * sp + i) for s in range(sec) for i in range(sp)]
    middle = lax.ppermute(quad, ("sec", "sp"), moves)
    sent, quad = lax.optimization_barrier((own_weight, quad))
    other_weight = lax.ppermute(sent, "tp", [(0, 1), (1, 0)])
    late, values = lax.optimization_barrier((late, values))
    late = to_heads(late)

    shift = jnp.where(lax.axis_index("sec") % 2 == 0, 2, sp - 2)
    turn = jnp.stack([lax.axis_index("sp"), shift]).astype(jnp.int32)
    text = project(turn, (quad, after, middle, behind), own_weight, other_weight, sp)
    part = (sp, half, head)
    early, text_out = attend(
        early_kernel, (part, (text.shape[0], head)), lengths, values, mixed, text, gate_scale
    )
    (image_heads,) = attend(
        late_kernel, ((sp, 2 * half, head),), lengths, values, mixed, text, gate_scale, late, early
    )
    image_out = to_heads(image_heads)
    return (image_out.transpose(1, 0, 2)[None], text_out[None, :, None, :])


def solution(mesh):
    in_specs = (
        P("sec", "sp", "tp"),
        P("tp", "sp", None),
        P(("sec", "tp"), "sp", None, None),
        P(None, "sp", None),
        P(("sec", "tp")),
        P(("sec", "tp")),
    )
    out_specs = (P(("sec", "tp"), "sp", None, None), P(("sec", "tp"), None, "sp", None))
    return jax.shard_map(shards, mesh=mesh, in_specs=in_specs, out_specs=out_specs, check_vma=False)
```
